128 devices in a mesh: row: 16 (over y, x), col: 8 (over z, core).
Axes of the slice: x: 4, y: 4, z: 4, core: 2. Of those that a mesh axis runs over, the one named last changes fastest.
Arguments:
- noise: float32 [512, 18, 2048], P('col', None, 'row'), may hold values from -6 to 6
- factor: bfloat16 [13, 2048, 3, 10240], P(None, 'row', None, 'col'), may hold values from -0.03125 to 0.03125
- dinv: bfloat16 [3, 10240, 5, 2048], P(None, 'col', None, 'row'), as said below
Outputs:
- solved: bfloat16 [3, 10240, 512], P(None, 'col')
- remaining: float32 [512, 18, 2048], P('col', None, 'row')
The draws below stay inside these ranges and needn't reach their ends.
Inputs may be any that keep to these rules, and one draw needn't show every extreme that they name: dinv[s], read as a 10240 x 10240 matrix, is lower triangular with a positive diagonal.
All inputs are finite; a program needn't handle non-finite values.
Results may differ from the reference program's by a relative error of at most 0.007.
Values may be sent and summed in bfloat16 or wider, within the bound.
No kernel may reach another device: no remote copies, remote signals or barrier semaphores. Data moves between devices by JAX's collectives and lax.ppermute only.
A program may use at most 128 MiB of HBM per device.

```python
import jax
import jax.numpy as jnp
from jax import lax

N = 36864
RHS = 512
RB = 128
STEPS = 3
PW = 10240
DR = 5
RBLK = 18
N_ROW = 16


def draw_dinv(key, part):
    key_off, key_diag = jax.random.split(jax.random.fold_in(key, 17))
    shape = (STEPS, PW, DR, N_ROW * RB)
    row_ids = lax.broadcasted_iota(jnp.int32, shape, 1)
    col_ids = lax.broadcasted_iota(jnp.int32, shape, 2) * (N_ROW * RB) + lax.broadcasted_iota(jnp.int32, shape, 3)
    offdiag = jax.random.normal(key_off, shape, jnp.float32)
    offdiag = offdiag * jnp.float32(PW) ** (-0.5)
    diagonal = jax.random.uniform(key_diag, shape, jnp.float32, 0.5, 1.5)
    values = jnp.where(col_ids < row_ids, offdiag, 0.0) + jnp.where(col_ids == row_ids, diagonal, 0.0)
    return values.astype(jnp.bfloat16)


def levels(key, extent, pieces, least, top_value):
    gain, own = 1.0, jax.random.fold_in(key, 6)
    for dim, shards_of in pieces:
        heights = jnp.exp(jax.random.uniform(jax.random.fold_in(own, dim), (shards_of,), jnp.float32, least / len(pieces), top_value / len(pieces)))
        gain = gain * jnp.repeat(heights, extent[dim] // shards_of).reshape([-1 if axis == dim else 1 for axis in range(len(extent))])
    return gain


def normal_values(own_key, shape, scale, reach, shards=(), kind=jnp.bfloat16):
    values = jax.random.normal(own_key, shape, jnp.float32) * scale
    if len(shards) > 0:
        values = levels(own_key, shape, shards, -0.22, 0.18) * values
    return jnp.clip(values, min=-reach, max=reach).astype(kind)


def setup_inputs(seed: int = 0) -> dict:
    key_of = jax.random.split(jax.random.key(seed), 4)
    return {
        "noise": normal_values(key_of[0], (RHS, RBLK, N_ROW * RB), 1.0, 6.0, ((0, 8), (2, 16)), jnp.float32),
        "factor": normal_values(key_of[1], (RBLK - DR, N_ROW * RB, STEPS, PW), (4 * PW) ** -0.5, 0.03125, ((1, 16), (3, 8))),
        "dinv": draw_dinv(jax.random.fold_in(key_of[3], 71), 0),
    }


def reference(noise, factor, dinv):
    width = PW
    work = noise.reshape(RHS, N).astype(jnp.float32)
    solved_list = []
    for step_idx in range(STEPS):
        current = work[:, step_idx * width:(step_idx + 1) * width].astype(jnp.bfloat16)
        inverse = dinv[step_idx].reshape(width, width).astype(jnp.float32)
        solution = jnp.dot(inverse, current.astype(jnp.float32).T, precision=lax.Precision.HIGHEST).astype(jnp.bfloat16)
        solved_list.append(solution)
        panel_rows = factor[:, :, step_idx, :].reshape((RBLK - DR) * N_ROW * RB, width)[step_idx * width:]
        update = jnp.dot(panel_rows.astype(jnp.float32), solution.astype(jnp.float32), precision=lax.Precision.HIGHEST)
        work = work.at[:, (step_idx + 1) * width:].add(-update.T)
    remaining = work.reshape(RHS, RBLK, N_ROW * RB)
    return jnp.stack(solved_list), remaining
```

```python
import jax
import jax.numpy as jnp
from jax import lax
from jax.sharding import PartitionSpec as P

BF16 = jnp.bfloat16
F32 = jnp.float32


def gather(block, axis, size):
    copies = jnp.broadcast_to(block[None], (size,) + block.shape)
    return lax.all_to_all(copies, axis, 0, 0, tiled=True)


def reduce_parts(parts, axis):
    received = lax.all_to_all(parts.astype(BF16), axis, 0, 0, tiled=True)
    return jnp.sum(received.astype(F32), axis=0)


def local(noise, factor, dinv):
    steps, width, rounds, lanes = dinv.shape
    n_row = lax.axis_size("row")
    n_col = lax.axis_size("col")
    total = noise.shape[1]
    vecs = noise.shape[0] * n_col
    solved_list = []
    done = [noise[:, :rounds, :]]
    current = noise[:, :rounds, :]
    for s in range(steps):
        everyone = lax.all_gather(current.astype(BF16), "col", axis=0, tiled=True)
        partial = lax.dot_general(
            dinv[s], everyone, (((1, 2), (1, 2)), ((), ())), preferred_element_type=F32
        )
        own = reduce_parts(partial.reshape(n_row, width // n_row, vecs), "row")
        solved = gather(own.astype(BF16), "row", n_row).reshape(width, vecs)
        solved_list.append(solved)
        first = (s + 1) * rounds
        last = min(first + rounds, total)
        update = 0.0
        for t in range(s + 1):
            update = update + lax.dot_general(
                solved_list[t],
                factor[first - rounds : last - rounds, :, t, :],
                (((0,), (2,)), ((), ())),
                preferred_element_type=F32,
            )
        reduced = reduce_parts(update.reshape(n_col, vecs // n_col, last - first, lanes), "col")
        current = noise[:, first:last, :] - reduced
        done.append(current)
    return jnp.stack(solved_list), jnp.concatenate(done, axis=1)


def solution(mesh):
    placed = (P("col", None, "row"), P(None, "row", None, "col"), P(None, "col", None, "row"))
    return jax.shard_map(
        local,
        mesh=mesh,
        in_specs=placed,
        out_specs=(P(None, "col", None), P("col", None, "row")),
        check_vma=False,
    )
```

```python
import jax
import jax.numpy as jnp
from jax import lax
from jax.sharding import PartitionSpec as P

BF16 = jnp.bfloat16
F32 = jnp.float32


def swap(block, n_col, mask):
    return lax.ppermute(block, "col", [(c, c ^ mask) for c in range(n_col)])


def same_core(n_col):
    return [[2 * z + k for z in range(n_col // 2)] for k in range(2)]


def tied(first, *others):
    return lax.optimization_barrier((first,) + others)


def product(solved, block):
    out = lax.dot_general(solved, block, (((1,), (2,)), ((), ())), preferred_element_type=F32)
    return out.transpose(1, 0, 2)


def local(noise, factor, dinv):
    steps, width, rounds, lanes = dinv.shape
    n_row = lax.axis_size("row")
    n_col = lax.axis_size("col")
    n_z = n_col // 2
    chunk, total, _ = noise.shape
    vecs = chunk * n_col
    half = vecs // 2
    my_z = lax.axis_index("col") // 2
    my_core = lax.axis_index("col") % 2
    noise = noise.transpose(1, 0, 2)
    bounds = [(s * rounds, min((s + 1) * rounds, total)) for s in range(steps + 1)]

    first = noise[:rounds].astype(BF16)
    copies = jnp.broadcast_to(first[None], (n_z,) + first.shape)
    own = lax.all_to_all(copies, "col", 0, 0, tiled=True, axis_index_groups=same_core(n_col))
    own = own.transpose(1, 0, 2, 3).reshape(rounds, half, lanes)
    done = [noise[:rounds]]
    solved_list = []
    later = {}
    for s in range(steps):
        other = swap(own, n_col, 1)
        everyone = jnp.concatenate([own, other], axis=1)
        partial = lax.dot_general(
            everyone, dinv[s], (((0, 2), (1, 2)), ((), ())), preferred_element_type=F32
        ).astype(BF16)
        parts = partial.reshape(n_row, vecs // n_row, width)
        received = lax.all_to_all(parts, "row", 0, 0, tiled=True)
        if s > 0:
            for n in range(s + 1, steps + 1):
                lo, hi = bounds[n]
                block = factor[lo - rounds : hi - rounds, :, s - 1, :]
                more = product(solved_list[s - 1], block)
                later[n] = more if n not in later else later[n] + more
            received, *held = tied(received, *[later[n] for n in range(s + 1, steps + 1)])
            later.update(zip(range(s + 1, steps + 1), held))
        mine = jnp.sum(received.astype(F32), axis=0).astype(BF16)
        copies = jnp.broadcast_to(mine[None], (n_row,) + mine.shape)
        solved = lax.all_to_all(copies, "row", 0, 0, tiled=True).reshape(vecs, width)
        solved_list.append(solved)

        lo, hi = bounds[s + 1]
        block = factor[lo - rounds : hi - rounds, :, s, :]
        update_other = product(solved[half:], block)
        if s > 0:
            update_other = update_other + later[s + 1][:, half:]
        arrived = swap(update_other.astype(BF16), n_col, 1)
        update = product(solved[:half], block)
        if s > 0:
            update = update + later[s + 1][:, :half]
        update = update + arrived.astype(F32)
        if s + 1 < steps:
            spread = update.reshape(hi - lo, n_z, chunk, lanes)
            here = (lax.iota(jnp.int32, n_z) == my_z)[None, :, None, None]
            work = (jnp.where(here, noise[lo:hi][:, None], 0.0) - spread).reshape(hi - lo, half, lanes)
            work = work + swap(work.astype(BF16), n_col, 2).astype(F32)
            work = work + swap(work.astype(BF16), n_col, n_col - 2).astype(F32)
            done.append(lax.dynamic_slice_in_dim(work, my_z * chunk, chunk, axis=1))
            own = work.astype(BF16)
        else:
            parts = update.astype(BF16).reshape(hi - lo, n_z, chunk, lanes).transpose(1, 0, 2, 3)
            got = lax.all_to_all(parts, "col", 0, 0, tiled=True, axis_index_groups=same_core(n_col))
            done.append(noise[lo:hi] - jnp.sum(got.astype(F32), axis=0))

    outs = []
    for solved in solved_list:
        halves = solved.reshape(2, n_z, chunk, width)
        ordered = jnp.where(my_core == 0, halves, halves[::-1])
        outs.append(ordered.transpose(3, 1, 0, 2).reshape(width, vecs))
    return jnp.stack(outs), jnp.concatenate(done, axis=0).transpose(1, 0, 2)


def solution(mesh):
    placed = (P("col", None, "row"), P(None, "row", None, "col"), P(None, "col", None, "row"))
    return jax.shard_map(
        local,
        mesh=mesh,
        in_specs=placed,
        out_specs=(P(None, "col", None), P("col", None, "row")),
        check_vma=False,
    )
```

```python
import jax
import jax.numpy as jnp
from jax import lax
from jax.experimental import pallas as pl
from jax.experimental.pallas import tpu as pltpu
from jax.sharding import PartitionSpec as P

BF16 = jnp.bfloat16
F32 = jnp.float32


def swap(block, n_col, masks):
    return lax.ppermute(block, "col", [(c, c ^ masks[c % 2]) for c in range(n_col)])


def place_kernel(core_ref, solved_ref, outs_ref, placed_ref):
    n_z, chunk = solved_ref.shape[1:3]
    own_first = core_ref[0] == 0
    for z in range(n_z):
        own = solved_ref[0, z]
        other = solved_ref[1, z]
        pair = jnp.concatenate([jnp.where(own_first, own, other), jnp.where(own_first, other, own)], axis=0)
        placed_ref[0, :, z * 2 * chunk : (z + 1) * 2 * chunk] = pair.T


def place(core, solved, outs, step, n_z):
    vecs, width = solved.shape
    tile = width // 5
    halves = solved.reshape(2, n_z, vecs // (2 * n_z), width)
    return pl.pallas_call(
        place_kernel,
        grid=(width // tile,),
        in_specs=[
            pl.BlockSpec(memory_space=pltpu.SMEM),
            pl.BlockSpec(halves.shape[:3] + (tile,), lambda i: (0, 0, 0, i)),
            pl.BlockSpec(memory_space=pl.ANY),
        ],
        out_specs=pl.BlockSpec((1, tile, vecs), lambda i: (step, i, 0)),
        out_shape=jax.ShapeDtypeStruct(outs.shape, outs.dtype),
        input_output_aliases={2: 0},
        cost_estimate=pl.CostEstimate(flops=0, bytes_accessed=4 * vecs * width, transcendentals=0),
    )(core, halves, outs)


def same_core(n_col):
    return [[2 * z + k for z in range(n_col // 2)] for k in range(2)]


def tied(first, *others):
    return lax.optimization_barrier((first,) + others)


def product(solved, block):
    out = lax.dot_general(solved, block, (((1,), (2,)), ((), ())), preferred_element_type=F32)
    return out.transpose(1, 0, 2)


def local(noise, factor, dinv):
    steps, width, rounds, lanes = dinv.shape
    n_row = lax.axis_size("row")
    n_col = lax.axis_size("col")
    n_z = n_col // 2
    chunk, total, _ = noise.shape
    vecs = chunk * n_col
    half = vecs // 2
    my_z = lax.axis_index("col") // 2
    core = (lax.axis_index("col") % 2).astype(jnp.int32).reshape(1)
    outs = jnp.zeros((steps, width, vecs), BF16)
    noise = noise.transpose(1, 0, 2)
    bounds = [(s * rounds, min((s + 1) * rounds, total)) for s in range(steps + 1)]

    first = noise[:rounds].astype(BF16)
    copies = jnp.broadcast_to(first[None], (n_z,) + first.shape)
    own = lax.all_to_all(copies, "col", 0, 0, tiled=True, axis_index_groups=same_core(n_col))
    own = own.transpose(1, 0, 2, 3).reshape(rounds, half, lanes)
    done = [noise[:rounds]]
    solved_list = []
    later = {}
    for s in range(steps):
        other = swap(own, n_col, (1, 1))
        everyone = jnp.concatenate([own, other], axis=1)
        partial = lax.dot_general(
            everyone, dinv[s], (((0, 2), (1, 2)), ((), ())), preferred_element_type=F32
        ).astype(BF16)
        parts = partial.reshape(n_row, vecs // n_row, width)
        received = lax.all_to_all(parts, "row", 0, 0, tiled=True)
        if s > 0:
            for n in range(s + 1, steps + 1):
                lo, hi = bounds[n]
                block = factor[lo - rounds : hi - rounds, :, s - 1, :]
                more = product(solved_list[s - 1], block)
                later[n] = more if n not in later else later[n] + more
            outs = place(core, solved_list[s - 1], outs, s - 1, n_z)
            received, outs, *held = tied(received, outs, *[later[n] for n in range(s + 1, steps + 1)])
            later.update(zip(range(s + 1, steps + 1), held))
        mine = jnp.sum(received.astype(F32), axis=0).astype(BF16)
        copies = jnp.broadcast_to(mine[None], (n_row,) + mine.shape)
        solved = lax.all_to_all(copies, "row", 0, 0, tiled=True).reshape(vecs, width)
        solved_list.append(solved)

        lo, hi = bounds[s + 1]
        block = factor[lo - rounds : hi - rounds, :, s, :]
        update_other = product(solved[half:], block)
        if s > 0:
            update_other = update_other + later[s + 1][:, half:]
        arrived = swap(update_other.astype(BF16), n_col, (1, 1))
        update = product(solved[:half], block)
        if s > 0:
            update = update + later[s + 1][:, :half]
        update = update + arrived.astype(F32)
        if s + 1 < steps:
            spread = update.reshape(hi - lo, n_z, chunk, lanes)
            here = (lax.iota(jnp.int32, n_z) == my_z)[None, :, None, None]
            work = (jnp.where(here, noise[lo:hi][:, None], 0.0) - spread).reshape(hi - lo, half, lanes)
            work = work + swap(work.astype(BF16), n_col, (2, n_col - 2)).astype(F32)
            work = work + swap(work.astype(BF16), n_col, (n_col - 2, 2)).astype(F32)
            done.append(lax.dynamic_slice_in_dim(work, my_z * chunk, chunk, axis=1))
            own = work.astype(BF16)
        else:
            parts = update.astype(BF16).reshape(hi - lo, n_z, chunk, lanes).transpose(1, 0, 2, 3)
            got = lax.all_to_all(parts, "col", 0, 0, tiled=True, axis_index_groups=same_core(n_col))
            done.append(noise[lo:hi] - jnp.sum(got.astype(F32), axis=0))

    outs = place(core, solved_list[-1], outs, steps - 1, n_z)
    return outs, jnp.concatenate(done, axis=0).transpose(1, 0, 2)


def solution(mesh):
    placed = (P("col", None, "row"), P(None, "row", None, "col"), P(None, "col", None, "row"))
    return jax.shard_map(
        local,
        mesh=mesh,
        in_specs=placed,
        out_specs=(P(None, "col", None), P("col", None, "row")),
        check_vma=False,
    )
```

```python
import jax
import jax.numpy as jnp
from jax import lax
from jax.experimental import pallas as pl
from jax.experimental.pallas import tpu as pltpu
from jax.sharding import PartitionSpec as P

BF16 = jnp.bfloat16
F32 = jnp.float32


class Places:
    def __init__(self):
        self.n_row = lax.axis_size("row")
        self.n_col = lax.axis_size("col")
        self.n_z = self.n_col // 2

    def column_groups(self):
        return [[2 * z + k for z in range(self.n_z)] for k in range(2)]

    def swap(self, block, masks):
        return lax.ppermute(block, "col", [(c, c ^ masks[c % 2]) for c in range(self.n_col)])


def tied(first, *others):
    return lax.optimization_barrier((first,) + others)


def add_up(parts):
    return jnp.sum(parts.astype(F32), axis=0)


def copies_of(block, count):
    return jnp.broadcast_to(block[None], (count,) + block.shape)


def place_kernel(core_ref, own_ref, other_ref, *refs):
    placed_ref = refs[-1]
    chunk = placed_ref.shape[2] // 8
    own_first = core_ref[0] == 0
    for z in range(own_ref.shape[0] // chunk):
        own = own_ref[z * chunk : (z + 1) * chunk]
        other = other_ref[z * chunk : (z + 1) * chunk]
        pair = jnp.concatenate([jnp.where(own_first, own, other), jnp.where(own_first, other, own)], axis=0)
        placed_ref[0, :, z * 2 * chunk : (z + 1) * 2 * chunk] = pair.T


def place(core, both, crossed, outs, step, steps):
    half, width = crossed.shape
    tile = width // 5
    block = pl.BlockSpec((half, tile), lambda i: (0, i))
    given = [core, both, crossed] + ([] if outs is None else [outs])
    return pl.pallas_call(
        place_kernel,
        grid=(width // tile,),
        in_specs=[pl.BlockSpec(memory_space=pltpu.SMEM), block, block] + [pl.BlockSpec(memory_space=pl.ANY)] * (len(given) - 3),
        out_specs=pl.BlockSpec((1, tile, 2 * half), lambda i: (step, i, 0)),
        out_shape=jax.ShapeDtypeStruct((steps, width, 2 * half), BF16),
        input_output_aliases={} if outs is None else {3: 0},
        cost_estimate=pl.CostEstimate(flops=0, bytes_accessed=8 * half * width, transcendentals=0),
    )(*given)


def inverse_times(current, inverse):
    return lax.dot_general(current, inverse, (((0, 2), (0, 2)), ((), ())), preferred_element_type=F32).astype(BF16)


def factor_times(solved, block):
    out = lax.dot_general(solved, block, (((1,), (2,)), ((), ())), preferred_element_type=F32)
    return out.transpose(1, 0, 2)


def local(noise, factor, dinv):
    steps, width, rounds, lanes = dinv.shape
    at = Places()
    n_z, n_col, n_row = at.n_z, at.n_col, at.n_row
    chunk, total, _ = noise.shape
    half = chunk * n_z
    my_z = lax.axis_index("col") // 2
    core = (lax.axis_index("col") % 2).astype(jnp.int32).reshape(1)
    noise = noise.transpose(1, 0, 2)
    dinv = dinv.transpose(0, 2, 1, 3).reshape(steps * rounds, width, lanes)
    factor = factor.transpose(0, 2, 1, 3).reshape(total - rounds, steps * lanes, width)
    bounds = [(s * rounds, min((s + 1) * rounds, total)) for s in range(steps + 1)]
    partner = (1, 1)

    dinv_theirs = at.swap(dinv, partner)
    first = noise[:rounds].astype(BF16)
    current = lax.all_to_all(copies_of(first, n_z), "col", 0, 0, tiled=True, axis_index_groups=at.column_groups())
    current = current.transpose(1, 0, 2, 3).reshape(rounds, half, lanes)
    done = [noise[:rounds]]
    later = {}
    outs = None
    solved = None
    for s in range(steps):
        lo, hi = bounds[s + 1]
        if s == 0:
            products = jnp.concatenate([inverse_times(current, dinv[:rounds]), inverse_times(current, dinv_theirs[:rounds])], axis=1)
            products, factor, noise = tied(products, factor, noise)
            factor_theirs = at.swap(factor, partner)
        else:
            products = inverse_times(current, inverse)
        products, before = tied(products, solved) if s > 0 else (products, None)
        received = lax.all_to_all(products.reshape(n_row, half // n_row, 2 * width), "row", 0, 0, tiled=True)
        if s > 0:
            for n in range(s + 1, steps + 1):
                start, end = bounds[n]
                for mine, source in enumerate((factor_theirs, factor)):
                    columns = before[:, :width] if mine else before[:, width:]
                    more = factor_times(columns, source[start - rounds : end - rounds, (s - 1) * lanes : s * lanes])
                    later[n] = more if n not in later else later[n] + more
            outs = place(core, before, at.swap(before[:, width:], partner), outs, s - 1, steps)
            received, outs, *held = tied(received, outs, *[later[n] for n in range(s + 1, steps + 1)])
            later.update(zip(range(s + 1, steps + 1), held))
        solved = jnp.sum(received.astype(F32), axis=0).astype(BF16)
        copies, factor, factor_theirs, dinv, dinv_theirs = tied(copies_of(solved, n_row), factor, factor_theirs, dinv, dinv_theirs)
        solved = lax.all_to_all(copies, "row", 0, 0, tiled=True)
        block = jnp.concatenate([f[lo - rounds : hi - rounds, s * lanes : (s + 1) * lanes] for f in (factor, factor_theirs)], axis=2)
        if s + 1 < steps:
            inverse = jnp.concatenate([d[(s + 1) * rounds : (s + 2) * rounds] for d in (dinv, dinv_theirs)], axis=1)
            solved, block, inverse = tied(solved, block, inverse)
        else:
            solved, block = tied(solved, block)
        solved = solved.reshape(half, 2 * width)

        update = factor_times(solved, block)
        if s > 0:
            update = update + later[s + 1]
        if s + 1 < steps:
            spread = update.reshape(hi - lo, n_z, chunk, lanes)
            here = (lax.iota(jnp.int32, n_z) == my_z)[None, :, None, None]
            work = (jnp.where(here, noise[lo:hi][:, None], 0.0) - spread).reshape(hi - lo, half, lanes)
            work = work + at.swap(work.astype(BF16), (2, n_col - 2)).astype(F32)
            work = work + at.swap(work.astype(BF16), (n_col - 2, 2)).astype(F32)
            done.append(lax.dynamic_slice_in_dim(work, my_z * chunk, chunk, axis=1))
            current = work.astype(BF16)
        else:
            parts = update.astype(BF16).reshape(hi - lo, n_z, chunk, lanes).transpose(1, 0, 2, 3)
            parts, last = tied(parts, solved)
            got = lax.all_to_all(parts, "col", 0, 0, tiled=True, axis_index_groups=at.column_groups())
            outs = place(core, last, at.swap(last[:, width:], partner), outs, s, steps)
            got, outs = tied(got, outs)
            done.append(noise[lo:hi] - add_up(got))
    return outs, jnp.concatenate(done, axis=0).transpose(1, 0, 2)


def solution(mesh):
    placed = (P("col", None, "row"), P(None, "row", None, "col"), P(None, "col", None, "row"))
    return jax.shard_map(
        local,
        mesh=mesh,
        in_specs=placed,
        out_specs=(P(None, "col", None), P("col", None, "row")),
        check_vma=False,
    )
```

```python
import jax
import jax.numpy as jnp
from jax import lax
from jax.experimental import pallas as pl
from jax.experimental.pallas import tpu as pltpu
from jax.sharding import PartitionSpec as P

BF16 = jnp.bfloat16
F32 = jnp.float32


class Places:
    def __init__(self):
        self.n_row = lax.axis_size("row")
        self.n_col = lax.axis_size("col")
        self.n_z = self.n_col // 2

    def column_groups(self):
        return [[2 * z + k for z in range(self.n_z)] for k in range(2)]

    def swap(self, block, masks):
        return lax.ppermute(block, "col", [(c, c ^ masks[c % 2]) for c in range(self.n_col)])


def tied(first, *others):
    return lax.optimization_barrier((first,) + others)


def add_up(parts):
    return jnp.sum(parts.astype(F32), axis=0)


def copies_of(block, count):
    return jnp.broadcast_to(block[None], (count,) + block.shape)


def place_kernel(core_ref, own_ref, other_ref, *refs):
    placed_ref = refs[-1]
    chunk = placed_ref.shape[2] // 8
    own_first = core_ref[0] == 0
    for z in range(own_ref.shape[0] // chunk):
        own = own_ref[z * chunk : (z + 1) * chunk]
        other = other_ref[z * chunk : (z + 1) * chunk]
        pair = jnp.concatenate([jnp.where(own_first, own, other), jnp.where(own_first, other, own)], axis=0)
        placed_ref[0, :, z * 2 * chunk : (z + 1) * 2 * chunk] = pair.T


def place(core, both, crossed, outs, step, steps):
    half, width = crossed.shape
    tile = width // 5
    block = pl.BlockSpec((half, tile), lambda i: (0, i))
    given = [core, both, crossed] + ([] if outs is None else [outs])
    return pl.pallas_call(
        place_kernel,
        grid=(width // tile,),
        in_specs=[pl.BlockSpec(memory_space=pltpu.SMEM), block, block] + [pl.BlockSpec(memory_space=pl.ANY)] * (len(given) - 3),
        out_specs=pl.BlockSpec((1, tile, 2 * half), lambda i: (step, i, 0)),
        out_shape=jax.ShapeDtypeStruct((steps, width, 2 * half), BF16),
        input_output_aliases={} if outs is None else {3: 0},
        cost_estimate=pl.CostEstimate(flops=0, bytes_accessed=8 * half * width, transcendentals=0),
    )(*given)


def join_kernel(*refs):
    count = len(refs) // 3
    for n in range(count):
        mine_ref, theirs_ref, out_ref = refs[2 * n], refs[2 * n + 1], refs[2 * count + n]
        rows, lanes = mine_ref.shape[1:]
        out_ref[0, :rows, :lanes] = mine_ref[0]
        out_ref[0, -rows:, -lanes:] = theirs_ref[0]


def joined(sources, pieces):
    given, in_specs, out_specs, shapes = [], [], [], []
    moved = 0
    for which, first, rounds, row, rows, axis in pieces:
        lanes = sources[which].shape[2]

        def block(i, first=first, rounds=rounds, row=row):
            return (first + jnp.minimum(i, rounds - 1), row, 0)

        def out_block(i, rounds=rounds):
            return (jnp.minimum(i, rounds - 1), 0, 0)

        shape = [rounds, rows, lanes]
        shape[axis] *= 2
        moved += 4 * shape[0] * shape[1] * shape[2]
        given += sources[which : which + 2]
        in_specs += [pl.BlockSpec((1, rows, lanes), block)] * 2
        out_specs.append(pl.BlockSpec((1, shape[1], shape[2]), out_block))
        shapes.append(jax.ShapeDtypeStruct(tuple(shape), BF16))
    return pl.pallas_call(
        join_kernel,
        grid=(max(piece[2] for piece in pieces),),
        in_specs=in_specs,
        out_specs=out_specs,
        out_shape=shapes,
        compiler_params=pltpu.CompilerParams(vmem_limit_bytes=32 * 2**20),
        cost_estimate=pl.CostEstimate(flops=0, bytes_accessed=moved, transcendentals=0),
    )(*given)


def inverse_times(current, inverse):
    return lax.dot_general(current, inverse, (((0, 2), (0, 2)), ((), ())), preferred_element_type=F32).astype(BF16)


def factor_times(solved, block):
    out = lax.dot_general(solved, block, (((1,), (2,)), ((), ())), preferred_element_type=F32)
    return out.transpose(1, 0, 2)


def local(noise, factor, dinv):
    steps, width, rounds, lanes = dinv.shape
    at = Places()
    n_z, n_col, n_row = at.n_z, at.n_col, at.n_row
    chunk, total, _ = noise.shape
    half = chunk * n_z
    my_z = lax.axis_index("col") // 2
    core = (lax.axis_index("col") % 2).astype(jnp.int32).reshape(1)
    noise = noise.transpose(1, 0, 2)
    dinv = dinv.transpose(0, 2, 1, 3).reshape(steps * rounds, width, lanes)
    factor = factor.transpose(0, 2, 1, 3).reshape(total - rounds, steps * lanes, width)
    bounds = [(s * rounds, min((s + 1) * rounds, total)) for s in range(steps + 1)]
    partner = (1, 1)

    dinv_theirs = at.swap(dinv, partner)
    first = noise[:rounds].astype(BF16)
    current = lax.all_to_all(copies_of(first, n_z), "col", 0, 0, tiled=True, axis_index_groups=at.column_groups())
    current = current.transpose(1, 0, 2, 3).reshape(rounds, half, lanes)
    done = []
    later = {}
    outs = None
    solved = None
    for s in range(steps):
        lo, hi = bounds[s + 1]
        if s == 0:
            products = jnp.concatenate([inverse_times(current, dinv[:rounds]), inverse_times(current, dinv_theirs[:rounds])], axis=1)
            products, factor, noise = tied(products, factor, noise)
            factor_theirs = at.swap(factor, partner)
        else:
            products = inverse_times(current, inverses[s])
        products, before = tied(products, solved) if s > 0 else (products, None)
        received = lax.all_to_all(products.reshape(n_row, half // n_row, 2 * width), "row", 0, 0, tiled=True)
        if s > 0:
            for n in range(s + 1, steps + 1):
                start, end = bounds[n]
                for mine, source in enumerate((factor_theirs, factor)):
                    columns = before[:, :width] if mine else before[:, width:]
                    more = factor_times(columns, source[start - rounds : end - rounds, (s - 1) * lanes : s * lanes])
                    later[n] = more if n not in later else later[n] + more
            outs = place(core, before, at.swap(before[:, width:], partner), outs, s - 1, steps)
            received, outs, *held = tied(received, outs, *[later[n] for n in range(s + 1, steps + 1)])
            later.update(zip(range(s + 1, steps + 1), held))
        solved = jnp.sum(received.astype(F32), axis=0).astype(BF16)
        copies = copies_of(solved, n_row)
        if s == 0:
            copies, factor, factor_theirs, dinv, dinv_theirs = tied(copies, factor, factor_theirs, dinv, dinv_theirs)
        solved = lax.all_to_all(copies, "row", 0, 0, tiled=True)
        if s == 0:
            pieces = [(0, t * rounds, hi - lo, t, lanes, 2) for t, (lo, hi) in enumerate(bounds[1:])]
            pieces += [(2, t * rounds, rounds, 0, width, 1) for t in range(1, steps)]
            held = joined((factor, factor_theirs, dinv, dinv_theirs), pieces)
            solved, *held = tied(solved, *held)
            blocks, inverses = held[:steps], [None] + held[steps:]
        solved = solved.reshape(half, 2 * width)

        update = factor_times(solved, blocks[s])
        if s > 0:
            update = update + later[s + 1]
        if s + 1 < steps:
            spread = update.reshape(hi - lo, n_z, chunk, lanes)
            here = (lax.iota(jnp.int32, n_z) == my_z)[None, :, None, None]
            work = (jnp.where(here, noise[lo:hi][:, None], 0.0) - spread).reshape(hi - lo, half, lanes)
            work = work + at.swap(work.astype(BF16), (2, n_col - 2)).astype(F32)
            work = work + at.swap(work.astype(BF16), (n_col - 2, 2)).astype(F32)
            done.append(lax.dynamic_slice_in_dim(work, my_z * chunk, chunk, axis=1))
            current = work.astype(BF16)
        else:
            parts = update.astype(BF16).reshape(hi - lo, n_z, chunk, lanes).transpose(1, 0, 2, 3)
            parts, last, noise = tied(parts, solved, noise)
            got = lax.all_to_all(parts, "col", 0, 0, tiled=True, axis_index_groups=at.column_groups())
            outs = place(core, last, at.swap(last[:, width:], partner), outs, s, steps)
            got, outs = tied(got, outs)
            done.append(noise[lo:hi] - add_up(got))
    return outs, jnp.concatenate([noise[:rounds]] + done, axis=0).transpose(1, 0, 2)


def solution(mesh):
    placed = (P("col", None, "row"), P(None, "row", None, "col"), P(None, "col", None, "row"))
    return jax.shard_map(
        local,
        mesh=mesh,
        in_specs=placed,
        out_specs=(P(None, "col", None), P("col", None, "row")),
        check_vma=False,
    )
```

```python
import jax
import jax.numpy as jnp
from jax import lax
from jax.experimental import pallas as pl
from jax.experimental.pallas import tpu as pltpu
from jax.sharding import PartitionSpec as P

BF16 = jnp.bfloat16
F32 = jnp.float32


class Places:
    def __init__(self):
        self.n_row = lax.axis_size("row")
        self.n_col = lax.axis_size("col")
        self.n_z = self.n_col // 2

    def column_groups(self):
        return [[2 * z + k for z in range(self.n_z)] for k in range(2)]

    def shift(self, block, hops):
        return lax.ppermute(block, "col", [(c, (c + 2 * hops) % self.n_col) for c in range(self.n_col)])

    def swap(self, block, masks):
        return lax.ppermute(block, "col", [(c, c ^ masks[c % 2]) for c in range(self.n_col)])


def tied(first, *others):
    return lax.optimization_barrier((first,) + others)


def copies_of(block, count):
    return jnp.broadcast_to(block[None], (count,) + block.shape)


def place_kernel(core_ref, own_ref, other_ref, *refs):
    placed_ref = refs[-1]
    chunk = placed_ref.shape[2] // 8
    own_first = core_ref[0] == 0
    for z in range(own_ref.shape[0] // chunk):
        own = own_ref[z * chunk : (z + 1) * chunk]
        other = other_ref[z * chunk : (z + 1) * chunk]
        pair = jnp.concatenate([jnp.where(own_first, own, other), jnp.where(own_first, other, own)], axis=0)
        placed_ref[0, :, z * 2 * chunk : (z + 1) * 2 * chunk] = pair.T


def place(core, both, crossed, outs, step, steps):
    half, width = both.shape[0], both.shape[1] // 2
    ahead = 5 * (crossed.shape[1] // width - 1)
    tile = width // 5
    block = pl.BlockSpec((half, tile), lambda i: (0, i))
    crossing = pl.BlockSpec((half, tile), lambda i: (0, ahead + i))
    given = [core, both, crossed] + ([] if outs is None else [outs])
    return pl.pallas_call(
        place_kernel,
        grid=(width // tile,),
        in_specs=[pl.BlockSpec(memory_space=pltpu.SMEM), block, crossing] + [pl.BlockSpec(memory_space=pl.ANY)] * (len(given) - 3),
        out_specs=pl.BlockSpec((1, tile, 2 * half), lambda i: (step, i, 0)),
        out_shape=jax.ShapeDtypeStruct((steps, width, 2 * half), BF16),
        input_output_aliases={} if outs is None else {3: 0},
        cost_estimate=pl.CostEstimate(flops=0, bytes_accessed=8 * half * width, transcendentals=0),
    )(*given)


def join_kernel(*refs):
    count = len(refs) // 3
    for n in range(count):
        mine_ref, theirs_ref, out_ref = refs[2 * n], refs[2 * n + 1], refs[2 * count + n]
        rows, lanes = mine_ref.shape[1:]
        out_ref[0, :rows, :lanes] = mine_ref[0]
        out_ref[0, -rows:, -lanes:] = theirs_ref[0]


def joined(sources, pieces):
    given, in_specs, out_specs, shapes = [], [], [], []
    moved = 0
    for which, first, rounds, row, rows, axis in pieces:
        lanes = sources[which].shape[2]

        def block(i, first=first, rounds=rounds, row=row):
            return (first + jnp.minimum(i, rounds - 1), row, 0)

        def out_block(i, rounds=rounds):
            return (jnp.minimum(i, rounds - 1), 0, 0)

        shape = [rounds, rows, lanes]
        shape[axis] *= 2
        moved += 4 * shape[0] * shape[1] * shape[2]
        given += sources[which : which + 2]
        in_specs += [pl.BlockSpec((1, rows, lanes), block)] * 2
        out_specs.append(pl.BlockSpec((1, shape[1], shape[2]), out_block))
        shapes.append(jax.ShapeDtypeStruct(tuple(shape), BF16))
    return pl.pallas_call(
        join_kernel,
        grid=(max(piece[2] for piece in pieces),),
        in_specs=in_specs,
        out_specs=out_specs,
        out_shape=shapes,
        compiler_params=pltpu.CompilerParams(vmem_limit_bytes=32 * 2**20),
        cost_estimate=pl.CostEstimate(flops=0, bytes_accessed=moved, transcendentals=0),
    )(*given)


def inverse_times(current, inverse):
    return lax.dot_general(current, inverse, (((0, 2), (0, 2)), ((), ())), preferred_element_type=F32).astype(BF16)


def factor_times(solved, block):
    out = lax.dot_general(solved, block, (((1,), (2,)), ((), ())), preferred_element_type=F32)
    return out.transpose(1, 0, 2)


def local(noise, factor, dinv):
    steps, width, rounds, lanes = dinv.shape
    at = Places()
    n_z, n_col, n_row = at.n_z, at.n_col, at.n_row
    chunk, total, _ = noise.shape
    half = chunk * n_z
    my_z = lax.axis_index("col") // 2
    core = (lax.axis_index("col") % 2).astype(jnp.int32).reshape(1)
    noise = noise.transpose(1, 0, 2)
    dinv = dinv.transpose(0, 2, 1, 3).reshape(steps * rounds, width, lanes)
    factor = factor.transpose(0, 2, 1, 3).reshape(total - rounds, steps * lanes, width)
    bounds = [(s * rounds, min((s + 1) * rounds, total)) for s in range(steps + 1)]
    partner = (1, 1)

    dinv_theirs = at.swap(dinv, partner)
    first = noise[:rounds].astype(BF16)
    current = lax.all_to_all(copies_of(first, n_z), "col", 0, 0, tiled=True, axis_index_groups=at.column_groups())
    current = current.transpose(1, 0, 2, 3).reshape(rounds, half, lanes)
    done = []
    later = {}
    outs = None
    solved = None
    for s in range(steps):
        lo, hi = bounds[s + 1]
        if s == 0:
            products = jnp.concatenate([inverse_times(current, dinv[:rounds]), inverse_times(current, dinv_theirs[:rounds])], axis=1)
            products, factor, noise = tied(products, factor, noise)
            factor_theirs = at.swap(factor, partner)
        else:
            products = inverse_times(current, inverses[s])
        products, before = tied(products, solved) if s > 0 else (products, None)
        received = lax.all_to_all(products.reshape(n_row, half // n_row, 2 * width), "row", 0, 0, tiled=True)
        if s > 0:
            for n in range(s + 1, steps + 1):
                start, end = bounds[n]
                for mine, source in enumerate((factor_theirs, factor)):
                    columns = before[:, :width] if mine else before[:, width:]
                    more = factor_times(columns, source[start - rounds : end - rounds, (s - 1) * lanes : s * lanes])
                    later[n] = more if n not in later else later[n] + more
            outs = place(core, before, at.swap(before[:, width:], partner), outs, s - 1, steps)
            received, outs, *held = tied(received, outs, *[later[n] for n in range(s + 1, steps + 1)])
            later.update(zip(range(s + 1, steps + 1), held))
            if s + 1 == steps:
                starts = [((my_z + hops) % n_z * chunk).astype(jnp.uint32) for hops in range(n_z)]
                received, *held = tied(received, noise[:rounds], *done, *starts)
                done, starts = held[:steps], held[steps:]
        solved = jnp.sum(received.astype(F32), axis=0).astype(BF16)
        copies = copies_of(solved, n_row)
        if s == 0:
            copies, factor, factor_theirs, dinv, dinv_theirs = tied(copies, factor, factor_theirs, dinv, dinv_theirs)
        solved = lax.all_to_all(copies, "row", 0, 0, tiled=True)
        if s == 0:
            pieces = [(0, t * rounds, hi - lo, t, lanes, 2) for t, (lo, hi) in enumerate(bounds[1:])]
            pieces += [(2, t * rounds, rounds, 0, width, 1) for t in range(1, steps)]
            held = joined((factor, factor_theirs, dinv, dinv_theirs), pieces)
            solved, *held = tied(solved, *held)
            blocks, inverses = held[:steps], [None] + held[steps:]
        solved = solved.reshape(half, 2 * width)

        update = factor_times(solved, blocks[s])
        if s > 0:
            update = update + later[s + 1]
        if s + 1 < steps:
            spread = update.reshape(hi - lo, n_z, chunk, lanes)
            here = (lax.iota(jnp.int32, n_z) == my_z)[None, :, None, None]
            work = (jnp.where(here, noise[lo:hi][:, None], 0.0) - spread).reshape(hi - lo, half, lanes)
            work = work + at.swap(work.astype(BF16), (2, n_col - 2)).astype(F32)
            work = work + at.swap(work.astype(BF16), (n_col - 2, 2)).astype(F32)
            done.append(lax.dynamic_slice_in_dim(work, my_z * chunk, chunk, axis=1))
            current = work.astype(BF16)
        else:
            pieces = [lax.dynamic_slice_in_dim(update, start, chunk, axis=1) for start in starts]
            sent = [piece.astype(BF16) for piece in pieces[1:]]
            last, noise, *sent = tied(solved, noise, *sent)
            got = [at.shift(piece, hops + 1) for hops, piece in enumerate(sent)]
            outs = place(core, last, at.swap(last, partner), outs, s, steps)
            outs, *got = tied(outs, *got)
            reduced = pieces[0]
            for part in got:
                reduced = reduced + part.astype(F32)
            done.append(noise[lo:hi] - reduced)
    return outs, jnp.concatenate(done, axis=0).transpose(1, 0, 2)


def solution(mesh):
    placed = (P("col", None, "row"), P(None, "row", None, "col"), P(None, "col", None, "row"))
    return jax.shard_map(
        local,
        mesh=mesh,
        in_specs=placed,
        out_specs=(P(None, "col", None), P("col", None, "row")),
        check_vma=False,
    )
```

```python
import jax
import jax.numpy as jnp
from jax import lax
from jax.experimental import pallas as pl
from jax.experimental.pallas import tpu as pltpu
from jax.sharding import PartitionSpec as P

BF16 = jnp.bfloat16
F32 = jnp.float32


class Places:
    def __init__(self):
        self.n_row = lax.axis_size("row")
        self.n_col = lax.axis_size("col")
        self.n_z = self.n_col // 2

    def column_groups(self):
        return [[2 * z + k for z in range(self.n_z)] for k in range(2)]

    def shift(self, block, hops):
        return lax.ppermute(block, "col", [(c, (c + 2 * hops) % self.n_col) for c in range(self.n_col)])

    def swap(self, block, masks):
        return lax.ppermute(block, "col", [(c, c ^ masks[c % 2]) for c in range(self.n_col)])


def tied(first, *others):
    return lax.optimization_barrier((first,) + others)


def copies_of(block, count):
    return jnp.broadcast_to(block[None], (count,) + block.shape)


def place_kernel(core_ref, own_ref, other_ref, *refs):
    placed_ref = refs[-1]
    chunk = placed_ref.shape[2] // 8
    own_first = core_ref[0] == 0
    for z in range(own_ref.shape[0] // chunk):
        own = own_ref[z * chunk : (z + 1) * chunk]
        other = other_ref[z * chunk : (z + 1) * chunk]
        pair = jnp.concatenate([jnp.where(own_first, own, other), jnp.where(own_first, other, own)], axis=0)
        placed_ref[0, :, z * 2 * chunk : (z + 1) * 2 * chunk] = pair.T


def place(core, both, crossed, outs, step, steps):
    half, width = both.shape[0], both.shape[1] // 2
    ahead = 5 * (crossed.shape[1] // width - 1)
    tile = width // 5
    block = pl.BlockSpec((half, tile), lambda i: (0, i))
    crossing = pl.BlockSpec((half, tile), lambda i: (0, ahead + i))
    given = [core, both, crossed] + ([] if outs is None else [outs])
    return pl.pallas_call(
        place_kernel,
        grid=(width // tile,),
        in_specs=[pl.BlockSpec(memory_space=pltpu.SMEM), block, crossing] + [pl.BlockSpec(memory_space=pl.ANY)] * (len(given) - 3),
        out_specs=pl.BlockSpec((1, tile, 2 * half), lambda i: (step, i, 0)),
        out_shape=jax.ShapeDtypeStruct((steps, width, 2 * half), BF16),
        input_output_aliases={} if outs is None else {3: 0},
        cost_estimate=pl.CostEstimate(flops=0, bytes_accessed=8 * half * width, transcendentals=0),
    )(*given)


def join_kernel(*refs):
    count = len(refs) // 3
    for n in range(count):
        mine_ref, theirs_ref, out_ref = refs[2 * n], refs[2 * n + 1], refs[2 * count + n]
        rows, lanes = mine_ref.shape[1:]
        at = pl.program_id(0) if out_ref.shape[0] > 1 else 0
        out_ref[at, :rows, :lanes] = mine_ref[0]
        out_ref[at, -rows:, -lanes:] = theirs_ref[0]


def joined(sources, pieces):
    given, in_specs, out_specs, shapes = [], [], [], []
    moved = 0
    for which, first, rounds, row, rows, axis in pieces:
        lanes = sources[which].shape[2]

        def block(i, first=first, rounds=rounds, row=row):
            return (first + jnp.minimum(i, rounds - 1), row, 0)

        def out_block(i, rounds=rounds):
            return (jnp.minimum(i, rounds - 1), 0, 0)

        shape = [rounds, rows, lanes]
        shape[axis] *= 2
        moved += 4 * shape[0] * shape[1] * shape[2]
        given += sources[which : which + 2]
        in_specs += [pl.BlockSpec((1, rows, lanes), block)] * 2
        if shapes:
            out_specs.append(pl.BlockSpec((1, shape[1], shape[2]), out_block))
            shapes.append(pltpu.HBM(tuple(shape), BF16))
        else:
            out_specs.append(pl.BlockSpec(memory_space=pltpu.VMEM))
            shapes.append(pltpu.VMEM(tuple(shape), BF16))
    return pl.pallas_call(
        join_kernel,
        grid=(max(piece[2] for piece in pieces),),
        in_specs=in_specs,
        out_specs=out_specs,
        out_shape=shapes,
        compiler_params=pltpu.CompilerParams(vmem_limit_bytes=32 * 2**20),
        cost_estimate=pl.CostEstimate(flops=0, bytes_accessed=moved, transcendentals=0),
    )(*given)


def inverse_times(current, inverse):
    return lax.dot_general(current, inverse, (((0, 2), (0, 2)), ((), ())), preferred_element_type=F32).astype(BF16)


def factor_times(solved, block):
    out = lax.dot_general(solved, block, (((1,), (2,)), ((), ())), preferred_element_type=F32)
    return out.transpose(1, 0, 2)


def local(noise, factor, dinv):
    steps, width, rounds, lanes = dinv.shape
    at = Places()
    n_z, n_col, n_row = at.n_z, at.n_col, at.n_row
    chunk, total, _ = noise.shape
    half = chunk * n_z
    my_z = lax.axis_index("col") // 2
    core = (lax.axis_index("col") % 2).astype(jnp.int32).reshape(1)
    noise = noise.transpose(1, 0, 2)
    dinv = dinv.transpose(0, 2, 1, 3).reshape(steps * rounds, width, lanes)
    factor = factor.transpose(0, 2, 1, 3).reshape(total - rounds, steps * lanes, width)
    bounds = [(s * rounds, min((s + 1) * rounds, total)) for s in range(steps + 1)]
    partner = (1, 1)

    dinv_theirs = at.swap(dinv, partner)
    first = noise[:rounds].astype(BF16)
    current = lax.all_to_all(copies_of(first, n_z), "col", 0, 0, tiled=True, axis_index_groups=at.column_groups())
    current = current.transpose(1, 0, 2, 3).reshape(rounds, half, lanes)
    done = []
    later = {}
    outs = None
    solved = None
    for s in range(steps):
        lo, hi = bounds[s + 1]
        if s == 0:
            products = jnp.concatenate([inverse_times(current, dinv[:rounds]), inverse_times(current, dinv_theirs[:rounds])], axis=1)
            products, factor, noise = tied(products, factor, noise)
            factor_theirs = at.swap(factor, partner)
        else:
            products = inverse_times(current, inverses[s])
        products, before = tied(products, solved) if s > 0 else (products, None)
        received = lax.all_to_all(products.reshape(n_row, half // n_row, 2 * width), "row", 0, 0, tiled=True)
        if s > 0:
            for n in range(s + 1, steps + 1):
                start, end = bounds[n]
                for mine, source in enumerate((factor_theirs, factor)):
                    columns = before[:, :width] if mine else before[:, width:]
                    more = factor_times(columns, source[start - rounds : end - rounds, (s - 1) * lanes : s * lanes])
                    later[n] = more if n not in later else later[n] + more
            outs = place(core, before, at.swap(before[:, width:], partner), outs, s - 1, steps)
            received, outs, *held = tied(received, outs, *[later[n] for n in range(s + 1, steps + 1)])
            later.update(zip(range(s + 1, steps + 1), held))
            if s + 1 == steps:
                starts = [((my_z + hops) % n_z * chunk).astype(jnp.uint32) for hops in range(n_z)]
                received, *held = tied(received, noise[:rounds], *done, *starts)
                done, starts = held[:steps], held[steps:]
        solved = jnp.sum(received.astype(F32), axis=0).astype(BF16)
        copies = copies_of(solved, n_row)
        if s == 0:
            copies, factor, factor_theirs, dinv, dinv_theirs = tied(copies, factor, factor_theirs, dinv, dinv_theirs)
        solved = lax.all_to_all(copies, "row", 0, 0, tiled=True)
        if s == 0:
            pieces = [(0, t * rounds, hi - lo, t, lanes, 2) for t, (lo, hi) in enumerate(bounds[1:])]
            pieces += [(2, t * rounds, rounds, 0, width, 1) for t in range(1, steps)]
            held = joined((factor, factor_theirs, dinv, dinv_theirs), pieces)
            solved, *held = tied(solved, *held)
            blocks, inverses = held[:steps], [None] + held[steps:]
        solved = solved.reshape(half, 2 * width)

        update = factor_times(solved, blocks[s])
        if s > 0:
            update = update + later[s + 1]
        if s + 1 < steps:
            spread = update.reshape(hi - lo, n_z, chunk, lanes)
            here = (lax.iota(jnp.int32, n_z) == my_z)[None, :, None, None]
            work = (jnp.where(here, noise[lo:hi][:, None], 0.0) - spread).reshape(hi - lo, half, lanes)
            work = work + at.swap(work.astype(BF16), (2, n_col - 2)).astype(F32)
            work = work + at.swap(work.astype(BF16), (n_col - 2, 2)).astype(F32)
            done.append(lax.dynamic_slice_in_dim(work, my_z * chunk, chunk, axis=1))
            current = work.astype(BF16)
        else:
            pieces = [lax.dynamic_slice_in_dim(update, start, chunk, axis=1) for start in starts]
            sent = [piece.astype(BF16) for piece in pieces[1:]]
            last, noise, *sent = tied(solved, noise, *sent)
            got = [at.shift(piece, hops + 1) for hops, piece in enumerate(sent)]
            outs = place(core, last, at.swap(last, partner), outs, s, steps)
            outs, *got = tied(outs, *got)
            reduced = pieces[0]
            for part in got:
                reduced = reduced + part.astype(F32)
            done.append(noise[lo:hi] - reduced)
    return outs, jnp.concatenate(done, axis=0).transpose(1, 0, 2)


def solution(mesh):
    placed = (P("col", None, "row"), P(None, "row", None, "col"), P(None, "col", None, "row"))
    return jax.shard_map(
        local,
        mesh=mesh,
        in_specs=placed,
        out_specs=(P(None, "col", None), P("col", None, "row")),
        check_vma=False,
    )
```
